32 devices in a mesh: fsdp: 2 (over y), context: 4 (over x, core), tensor: 4 (over z).
Axes of the slice: x: 2, y: 2, z: 4, core: 2. Of those that a mesh axis runs over, the one named last changes fastest.
Arguments:
- inputs: bfloat16 [4096, 1024], P(('fsdp', 'context')), may hold values from -6 to 6
- cotangent: bfloat16 [4096, 1024], P(('fsdp', 'context')), may hold values from -6 to 6
- lengths: int32 [2, 4], P('fsdp'), may hold values from 1 to 2048, as said below
- w_query: float32 [1024, 1024], P(('fsdp', 'context'), 'tensor'), may hold values from -0.1875 to 0.1875
- w_key: float32 [1024, 512], P(('fsdp', 'context'), 'tensor'), may hold values from -0.1875 to 0.1875
- w_value: float32 [1024, 512], P(('fsdp', 'context'), 'tensor'), may hold values from -0.1875 to 0.1875
- w_out: float32 [1024, 1024], P(('fsdp', 'context'), 'tensor'), may hold values from -1.5 to 1.5
- w_gate: float32 [1024, 4608], P(('fsdp', 'context'), 'tensor'), may hold values from -0.1875 to 0.1875
- w_up: float32 [1024, 4608], P(('fsdp', 'context'), 'tensor'), may hold values from -0.1875 to 0.1875
- w_down: float32 [1024, 4608], P(('fsdp', 'context'), 'tensor'), may hold values from -0.09375 to 0.09375
- m_query: float32 [1024, 1024], P(('fsdp', 'context'), 'tensor'), may hold values from -192 to 192
- m_key: float32 [1024, 512], P(('fsdp', 'context'), 'tensor'), may hold values from -192 to 192
- m_value: float32 [1024, 512], P(('fsdp', 'context'), 'tensor'), may hold values from -192 to 192
- m_out: float32 [1024, 1024], P(('fsdp', 'context'), 'tensor'), may hold values from -80 to 80
- m_gate: float32 [1024, 4608], P(('fsdp', 'context'), 'tensor'), may hold values from -112 to 112
- m_up: float32 [1024, 4608], P(('fsdp', 'context'), 'tensor'), may hold values from -112 to 112
- m_down: float32 [1024, 4608], P(('fsdp', 'context'), 'tensor'), may hold values from -224 to 224
- gains: float32 [2176], replicated, may hold values from 0.5 to 1.5
- gain_moment: float32 [2176], replicated, may hold values from -384 to 384
Outputs:
- block_out: bfloat16 [4096, 1024], P(('fsdp', 'context'))
- input_grad: float32 [4096, 1024], P(('fsdp', 'context'))
- mom_query: float32 [1024, 1024], P(('fsdp', 'context'), 'tensor')
- mom_key: float32 [1024, 512], P(('fsdp', 'context'), 'tensor')
- mom_value: float32 [1024, 512], P(('fsdp', 'context'), 'tensor')
- mom_out: float32 [1024, 1024], P(('fsdp', 'context'), 'tensor')
- mom_gate: float32 [1024, 4608], P(('fsdp', 'context'), 'tensor')
- mom_up: float32 [1024, 4608], P(('fsdp', 'context'), 'tensor')
- mom_down: float32 [1024, 4608], P(('fsdp', 'context'), 'tensor')
- new_query: float32 [1024, 1024], P(('fsdp', 'context'), 'tensor')
- new_key: float32 [1024, 512], P(('fsdp', 'context'), 'tensor')
- new_value: float32 [1024, 512], P(('fsdp', 'context'), 'tensor')
- new_out: float32 [1024, 1024], P(('fsdp', 'context'), 'tensor')
- new_gate: float32 [1024, 4608], P(('fsdp', 'context'), 'tensor')
- new_up: float32 [1024, 4608], P(('fsdp', 'context'), 'tensor')
- new_down: float32 [1024, 4608], P(('fsdp', 'context'), 'tensor')
- gain_mom: float32 [2176], replicated
- new_gains: float32 [2176], replicated
The draws below stay inside these ranges and needn't reach their ends.
Inputs may be any that keep to these rules, and one draw needn't show every extreme that they name: `lengths`: each row sums to 2048; one sequence of each row starts among the first quarter of the stream's tokens and ends in the last quarter.
All inputs are finite; a program needn't handle non-finite values.
Results may differ from the reference program's by a relative error of at most 0.028.
Values may be sent and summed in bfloat16 or wider, within the bound.
A program may use at most 128 MiB of HBM per device.

```python
import math
import jax
import jax.numpy as jnp
from jax import lax

D = 1024
HEADS = 16
KV_HEADS = 8
HD = 64
FF = 4608
NSEQ = 4
NS_STEPS = 5
GROUP_TOK = 2048
TOKENS = 4096
GAINS = 2176
N_FSDP = 2


def draw_lengths(key, part):
    key = jax.random.fold_in(key, 11)
    limit = GROUP_TOK // (4 * (NSEQ - 1))
    smalls = jax.random.randint(jax.random.fold_in(key, 1), (N_FSDP, NSEQ), 1, limit)
    chosen = jax.random.randint(jax.random.fold_in(key, 2), (N_FSDP, 1), 0, NSEQ)
    slots = jnp.arange(NSEQ, dtype=jnp.int32)[None, :]
    others = jnp.sum(jnp.where(slots == chosen, 0, smalls), axis=1, keepdims=True)
    longest = GROUP_TOK - others
    return jnp.where(slots == chosen, longest, smalls).astype(jnp.int32)


def shard_levels(own_key, dims, cuts, low, largest):
    loudness = 1.0
    for position, parts in cuts:
        draws = jax.random.uniform(jax.random.fold_in(jax.random.fold_in(own_key, 6), position), (parts,), jnp.float32, low / len(cuts), largest / len(cuts))
        loudness = loudness * jnp.repeat(jnp.exp(draws), dims[position] // parts).reshape((-1,) + (1,) * (len(dims) - 1 - position))
    return loudness


def centred(own_key, dims, spread, bound, cuts=(), kind=jnp.bfloat16):
    entries = jax.random.normal(own_key, dims, jnp.float32) * spread
    if len(cuts) > 0:
        entries = shard_levels(own_key, dims, cuts, -0.22, 0.18) * entries
    return jnp.clip(entries, min=-bound, max=bound).astype(kind)


def setup_inputs(seed: int = 0) -> dict:
    arg_keys = jax.random.split(jax.random.key(seed), 20)
    return {
        "inputs": centred(arg_keys[0], (TOKENS, D), 1.0, 6.0, ((0, 8),)),
        "cotangent": centred(arg_keys[1], (TOKENS, D), 1.0, 6.0, ((0, 8),)),
        "lengths": draw_lengths(jax.random.fold_in(arg_keys[19], 71), 0),
        "w_query": centred(arg_keys[3], (D, HEADS * HD), D ** -0.5, 0.1875, ((0, 8), (1, 4)), jnp.float32),
        "w_key": centred(arg_keys[4], (D, KV_HEADS * HD), D ** -0.5, 0.1875, ((0, 8), (1, 4)), jnp.float32),
        "w_value": centred(arg_keys[5], (D, KV_HEADS * HD), D ** -0.5, 0.1875, ((0, 8), (1, 4)), jnp.float32),
        "w_out": centred(arg_keys[6], (D, HEADS * HD), (HD // 4) ** -0.5, 1.5, ((0, 8), (1, 4)), jnp.float32),
        "w_gate": centred(arg_keys[7], (D, FF), D ** -0.5, 0.1875, ((0, 8), (1, 4)), jnp.float32),
        "w_up": centred(arg_keys[8], (D, FF), D ** -0.5, 0.1875, ((0, 8), (1, 4)), jnp.float32),
        "w_down": centred(arg_keys[9], (D, FF), FF ** -0.5, 0.09375, ((0, 8), (1, 4)), jnp.float32),
        "m_query": centred(arg_keys[10], (D, HEADS * HD), (0.5 * TOKENS ** 0.5), 192.0, ((0, 8), (1, 4)), jnp.float32),
        "m_key": centred(arg_keys[11], (D, KV_HEADS * HD), (0.5 * TOKENS ** 0.5), 192.0, ((0, 8), (1, 4)), jnp.float32),
        "m_value": centred(arg_keys[12], (D, KV_HEADS * HD), (0.5 * TOKENS ** 0.5), 192.0, ((0, 8), (1, 4)), jnp.float32),
        "m_out": centred(arg_keys[13], (D, HEADS * HD), (0.2 * TOKENS ** 0.5), 80.0, ((0, 8), (1, 4)), jnp.float32),
        "m_gate": centred(arg_keys[14], (D, FF), (0.3 * TOKENS ** 0.5), 112.0, ((0, 8), (1, 4)), jnp.float32),
        "m_up": centred(arg_keys[15], (D, FF), (0.3 * TOKENS ** 0.5), 112.0, ((0, 8), (1, 4)), jnp.float32),
        "m_down": centred(arg_keys[16], (D, FF), (0.6 * TOKENS ** 0.5), 224.0, ((0, 8), (1, 4)), jnp.float32),
        "gains": jnp.clip(1.0 + 0.1 * jax.random.normal(arg_keys[17], (GAINS,), jnp.float32), 0.5, 1.5),
        "gain_moment": centred(arg_keys[18], (GAINS,), (TOKENS ** 0.5), 384.0, (), jnp.float32),
    }


EPS = 1e-06
THETA = 1000000.0
MU = 0.95
MU_G = 0.9
LR_G = 0.001
NS_A = 3.4445
NS_B = -4.775
NS_C = 2.0315
RATES = (0.1, 0.1, 0.1, 0.8, 0.1, 0.1, 0.1)
HIGH = lax.Precision.HIGHEST

@jax.custom_vjp
def low(v):
    return lax.optimization_barrier(v.astype(jnp.bfloat16)).astype(jnp.float32)

@jax.custom_vjp
def low_back(v):
    return v

def low_keep(v):
    return (low(v), None)

def low_pass(kept, grad):
    return (grad,)

def back_keep(v):
    return (v, None)

def back_low(kept, grad):
    return (low(grad),)
low.defvjp(low_keep, low_pass)
low_back.defvjp(back_keep, back_low)

def rms_scale(values):
    return lax.rsqrt(lax.optimization_barrier(jnp.mean(values * values, axis=-1, keepdims=True)) + EPS)

def rotate(values, cosines, sines_table):
    half_dim = values.shape[-1] // 2
    front_half = values[..., :half_dim]
    back_half = values[..., half_dim:]
    cos_rows = cosines[:, None, :]
    sin_rows = sines_table[:, None, :]
    return jnp.concatenate([front_half * cos_rows - back_half * sin_rows, back_half * cos_rows + front_half * sin_rows], axis=-1)

def stream_layout(row_lengths, points):
    ends = jnp.cumsum(row_lengths).astype(jnp.int32)
    after = (points[:, None] >= ends[None, :]).astype(jnp.int32)
    segment = lax.optimization_barrier(jnp.sum(after, axis=1)).astype(jnp.int32)
    place = (points - lax.optimization_barrier(jnp.sum(after * row_lengths[None, :], axis=1))).astype(jnp.int32)
    return (segment, place)

def rope_tables(place):
    freq = THETA ** (-(2.0 * jnp.arange(HD // 2, dtype=jnp.float32)) / HD)
    angles = place.astype(jnp.float32)[:, None] * freq[None, :]
    return (jnp.cos(angles), jnp.sin(angles))

def newton_schulz(matrix, pieces):
    wide = matrix.astype(jnp.float32)
    frob_norm = jnp.sqrt(jnp.sum(wide * wide))
    current = (wide / (frob_norm + 1e-07)).astype(jnp.bfloat16)
    column_width = current.shape[1] // pieces
    for repeat in range(NS_STEPS):
        square = jnp.dot(current, current.T, preferred_element_type=jnp.float32).astype(jnp.bfloat16)
        quartic = jnp.dot(square, square, preferred_element_type=jnp.float32)
        mixer = (NS_B * square.astype(jnp.float32) + NS_C * quartic).astype(jnp.bfloat16)
        columns = []
        for column_index in range(pieces):
            column = current[:, column_index * column_width:(column_index + 1) * column_width]
            columns.append((NS_A * column.astype(jnp.float32) + jnp.dot(mixer, column, preferred_element_type=jnp.float32)).astype(jnp.bfloat16))
        current = jnp.concatenate(columns, axis=1)
    return current

def group_forward(rows, halves, gain_vec, row_lengths):
    w_q, w_k, w_v, w_o, w_g, w_u, w_d = halves
    gain_one = gain_vec[:D]
    gain_two = gain_vec[D:2 * D]
    gain_query = gain_vec[2 * D:2 * D + HD]
    gain_key = gain_vec[2 * D + HD:]
    span = rows.shape[0]
    points = jnp.arange(span, dtype=jnp.int32)
    segment, place = stream_layout(row_lengths, points)
    allowed = (segment[:, None] == segment[None, :]) & (points[None, :] <= points[:, None])
    cosines, sines_table = rope_tables(place)
    normed = low(rows * rms_scale(rows) * gain_one)
    query = low_back(jnp.dot(normed, w_q, precision=HIGH)).reshape(span, HEADS, HD)
    keys = low_back(jnp.dot(normed, w_k, precision=HIGH)).reshape(span, KV_HEADS, HD)
    values = low(low_back(jnp.dot(normed, w_v, precision=HIGH))).reshape(span, KV_HEADS, HD)
    query = low(rotate(query * rms_scale(query) * gain_query, cosines, sines_table))
    keys = low(rotate(keys * rms_scale(keys) * gain_key, cosines, sines_table))
    group_size = HEADS // KV_HEADS
    query_by = query.reshape(span, KV_HEADS, group_size, HD).transpose(1, 2, 0, 3)
    keys_by = keys.transpose(1, 0, 2)
    values_by = values.transpose(1, 0, 2)
    scale = HD ** (-0.5)

    def one_head(bundle):
        head_q, head_k, head_v = bundle
        scores = low_back(jnp.einsum('gtd,sd->gts', head_q, head_k, precision=HIGH) * scale)
        scores = jnp.where(allowed[None], scores, -1e+30)
        probs = low(jax.nn.softmax(scores, axis=-1))
        return low(low_back(jnp.einsum('gts,sd->gtd', probs, head_v, precision=HIGH)))
    mixed = lax.map(jax.checkpoint(one_head), (query_by, keys_by, values_by))
    mixed = mixed.transpose(2, 0, 1, 3).reshape(span, HEADS * HD)
    attended = low_back(jnp.dot(mixed, w_o.T, precision=HIGH))
    resid = rows + attended
    second = low(resid * rms_scale(resid) * gain_two)
    gate = low_back(jnp.dot(second, w_g, precision=HIGH))
    up_proj = low_back(jnp.dot(second, w_u, precision=HIGH))
    hidden = low(jax.nn.silu(gate) * up_proj)
    return resid + jnp.dot(hidden, w_d.T, precision=HIGH)

def reference(inputs, cotangent, lengths, w_query, w_key, w_value, w_out, w_gate, w_up, w_down, m_query, m_key, m_value, m_out, m_gate, m_up, m_down, gains, gain_moment):
    masters = (w_query, w_key, w_value, w_out, w_gate, w_up, w_down)
    moments = (m_query, m_key, m_value, m_out, m_gate, m_up, m_down)
    rows_all = inputs.astype(jnp.float32).reshape(N_FSDP, GROUP_TOK, D)
    cot_all = cotangent.astype(jnp.float32).reshape(N_FSDP, GROUP_TOK, D)

    def forward(params, gain_vec, stream_rows):
        halves = tuple((low(weight) for weight in params))
        return lax.map(lambda bundle: group_forward(bundle[0], halves, gain_vec, bundle[1]), (stream_rows, lengths))
    outcome, pullback = jax.vjp(forward, masters, gains, rows_all)
    grads, gain_grad, row_grad = pullback(cot_all)
    block_out = outcome.reshape(TOKENS, D).astype(jnp.bfloat16)
    input_grad = row_grad.reshape(TOKENS, D)
    new_moments = tuple((MU * moment_old + gradient for moment_old, gradient in zip(moments, grads)))
    new_weights = []
    for index in range(len(RATES)):
        ortho = newton_schulz(new_moments[index].astype(jnp.bfloat16), 1)
        columns = masters[index].shape[1]
        rate = RATES[index] * 0.2 * math.sqrt(max(D, columns))
        new_weights.append(masters[index] - rate * ortho.astype(jnp.float32))
    gain_mom = MU_G * gain_moment + gain_grad
    new_gains = gains - LR_G * gain_mom
    return (block_out, input_grad, new_moments[0], new_moments[1], new_moments[2], new_moments[3], new_moments[4], new_moments[5], new_moments[6], new_weights[0], new_weights[1], new_weights[2], new_weights[3], new_weights[4], new_weights[5], new_weights[6], gain_mom, new_gains)
```

```python
import math

import jax
import jax.numpy as jnp
from jax import lax
from jax.sharding import PartitionSpec as P

D = 1024
HEADS = 16
KV_HEADS = 8
HD = 64
NS_STEPS = 5


EPS = 1e-06
THETA = 1000000.0
MU = 0.95
MU_G = 0.9
LR_G = 0.001
NS_A = 3.4445
NS_B = -4.775
NS_C = 2.0315
RATES = (0.1, 0.1, 0.1, 0.8, 0.1, 0.1, 0.1)
FULL_TYPE = jnp.float32
HALF_TYPE = jnp.bfloat16


def rms_scale(values):
    return lax.rsqrt(jnp.mean(values * values, axis=-1, keepdims=True) + EPS)


def rotate(values, cosines, sines_table):
    half_dim = values.shape[-1] // 2
    front_half = values[..., :half_dim]
    back_half = values[..., half_dim:]
    cos_rows = cosines[:, None, :]
    sin_rows = sines_table[:, None, :]
    return jnp.concatenate(
        [
            front_half * cos_rows - back_half * sin_rows,
            back_half * cos_rows + front_half * sin_rows,
        ],
        axis=-1,
    )


def rotate_back(values, cosines, sines_table):
    half_dim = values.shape[-1] // 2
    front_half = values[..., :half_dim]
    back_half = values[..., half_dim:]
    cos_rows = cosines[:, None, :]
    sin_rows = sines_table[:, None, :]
    return jnp.concatenate(
        [
            front_half * cos_rows + back_half * sin_rows,
            back_half * cos_rows - front_half * sin_rows,
        ],
        axis=-1,
    )


def norm_back(upstream, unit_rows, scale_rows, gain_row):
    scaled = upstream * gain_row
    return scale_rows * (scaled - unit_rows * jnp.mean(scaled * unit_rows, axis=-1, keepdims=True))


def stream_layout(row_lengths, points):
    ends = jnp.cumsum(row_lengths)
    after = (points[:, None] >= ends[None, :]).astype(jnp.int32)
    segment = jnp.sum(after, axis=1)
    place = points - jnp.sum(after * row_lengths[None, :], axis=1)
    return (segment, place)


def rope_tables(place):
    freq = THETA ** (-(2.0 * jnp.arange(HD // 2, dtype=FULL_TYPE)) / HD)
    angles = place.astype(FULL_TYPE)[:, None] * freq[None, :]
    return (jnp.cos(angles), jnp.sin(angles))


def newton_schulz(matrix):
    wide = matrix.astype(FULL_TYPE)
    frob_norm = jnp.sqrt(jnp.sum(wide * wide))
    current = (wide / (frob_norm + 1e-07)).astype(HALF_TYPE)
    for repeat in range(NS_STEPS):
        square = lax.dot_general(
            current, current, (((1,), (1,)), ((), ())), preferred_element_type=FULL_TYPE
        ).astype(HALF_TYPE)
        quartic = jnp.dot(square, square, preferred_element_type=FULL_TYPE)
        mixer = (NS_B * square.astype(FULL_TYPE) + NS_C * quartic).astype(HALF_TYPE)
        current = (
            NS_A * current.astype(FULL_TYPE)
            + jnp.dot(mixer, current, preferred_element_type=FULL_TYPE)
        ).astype(HALF_TYPE)
    return current


def gram_newton_schulz(gram_half):
    gram = gram_half.astype(FULL_TYPE)
    size = gram.shape[0]
    diagonal = jnp.arange(size)[:, None] == jnp.arange(size)[None, :]
    norm = jnp.sqrt(jnp.sum(jnp.where(diagonal, gram, 0.0))) + 1e-07
    inverse = 1.0 / norm
    gram = gram * inverse * inverse
    total = None
    for repeat in range(NS_STEPS):
        half = gram.astype(HALF_TYPE)
        mixer_full = NS_B * gram + NS_C * jnp.dot(half, half, preferred_element_type=FULL_TYPE)
        mixer = mixer_full.astype(HALF_TYPE)
        if total is None:
            total = jnp.where(diagonal, NS_A, 0.0) + mixer_full
        else:
            total = NS_A * total + jnp.dot(
                mixer, total.astype(HALF_TYPE), preferred_element_type=FULL_TYPE
            )
        if repeat < NS_STEPS - 1:
            once = NS_A * gram + jnp.dot(mixer, half, preferred_element_type=FULL_TYPE)
            gram = NS_A * once + jnp.dot(
                once.astype(HALF_TYPE), mixer, preferred_element_type=FULL_TYPE
            )
    return (total * inverse).astype(HALF_TYPE)


def head_rows(values, head_index, group_size):
    picked = values[:, head_index * group_size : (head_index + 1) * group_size, :]
    return picked.transpose(1, 0, 2).reshape(group_size * values.shape[0], values.shape[2])


def body(
    inputs,
    cotangent,
    lengths,
    w_query,
    w_key,
    w_value,
    w_out,
    w_gate,
    w_up,
    w_down,
    m_query,
    m_key,
    m_value,
    m_out,
    m_gate,
    m_up,
    m_down,
    gains,
    gain_moment,
):
    masters = (w_query, w_key, w_value, w_out, w_gate, w_up, w_down)
    moments = (m_query, m_key, m_value, m_out, m_gate, m_up, m_down)
    rows_here = inputs.shape[0]
    context_size = lax.axis_size("context")
    tensor_size = lax.axis_size("tensor")
    span = context_size * rows_here
    offset = lax.axis_index("context") * rows_here
    local_q = w_query.shape[1] // HD
    local_kv = w_key.shape[1] // HD
    group_size = HEADS // KV_HEADS
    scale = HD ** (-0.5)
    gain_one = gains[:D]
    gain_two = gains[D : 2 * D]
    gain_query = gains[2 * D : 2 * D + HD]
    gain_key = gains[2 * D + HD :]
    points = jnp.arange(span, dtype=jnp.int32)
    segment, place = stream_layout(lengths[0], points)
    query_points = offset + jnp.arange(rows_here, dtype=jnp.int32)
    query_segment = lax.dynamic_slice_in_dim(segment, offset, rows_here)
    query_place = lax.dynamic_slice_in_dim(place, offset, rows_here)
    allowed = (query_segment[:, None] == segment[None, :]) & (
        points[None, :] <= query_points[:, None]
    )
    allowed_rows = jnp.concatenate([allowed] * group_size, axis=0)
    cosines, sines_table = rope_tables(query_place)
    half_q = w_query.astype(HALF_TYPE)
    half_k = w_key.astype(HALF_TYPE)
    half_v = w_value.astype(HALF_TYPE)
    half_o = w_out.astype(HALF_TYPE)
    half_g = w_gate.astype(HALF_TYPE)
    half_u = w_up.astype(HALF_TYPE)
    half_d = w_down.astype(HALF_TYPE)
    plane = ("fsdp", "context")
    width_q, width_k, width_f = w_query.shape[1], w_key.shape[1], w_gate.shape[1]
    full_qkv = lax.all_gather(
        jnp.concatenate([half_q, half_k, half_v], axis=1), plane, axis=0, tiled=True
    )
    full_o = lax.all_gather(half_o, plane, axis=0, tiled=True)
    full_gu = lax.all_gather(
        jnp.concatenate([half_g, half_u], axis=1), plane, axis=0, tiled=True
    )
    full_d = lax.all_gather(half_d, plane, axis=0, tiled=True)
    rows = inputs.astype(FULL_TYPE)
    scale_one = rms_scale(rows)
    unit_one = rows * scale_one
    normed = (unit_one * gain_one).astype(HALF_TYPE)
    qkv_raw = jnp.dot(normed, full_qkv, preferred_element_type=FULL_TYPE)
    query_raw = qkv_raw[:, :width_q].reshape(rows_here, local_q, HD)
    key_raw = qkv_raw[:, width_q : width_q + width_k].reshape(rows_here, local_kv, HD)
    value_half = qkv_raw[:, width_q + width_k :].astype(HALF_TYPE)
    scale_q = rms_scale(query_raw)
    unit_q = query_raw * scale_q
    query_half = rotate(unit_q * gain_query, cosines, sines_table).astype(HALF_TYPE)
    scale_k = rms_scale(key_raw)
    unit_k = key_raw * scale_k
    key_half = rotate(unit_k * gain_key, cosines, sines_table).astype(HALF_TYPE)
    key_value = lax.all_gather(
        jnp.concatenate([key_half.reshape(rows_here, local_kv * HD), value_half], axis=1),
        "context",
        axis=0,
        tiled=True,
    )
    key_all = key_value[:, :width_k]
    value_all = key_value[:, width_k:]

    def head_scores(query_rows, key_cols):
        scores = (
            jnp.einsum("qd,kd->qk", query_rows, key_cols, preferred_element_type=FULL_TYPE) * scale
        )
        return jnp.where(allowed_rows, scores, -1e30)

    mixed_parts = []
    lse_parts = []
    for head_index in range(local_kv):
        query_rows = head_rows(query_half, head_index, group_size)
        key_cols = key_all[:, head_index * HD : (head_index + 1) * HD]
        value_cols = value_all[:, head_index * HD : (head_index + 1) * HD]
        scores = head_scores(query_rows, key_cols)
        peak = jnp.max(scores, axis=-1, keepdims=True)
        expo = jnp.exp(scores - peak)
        denom = jnp.sum(expo, axis=-1, keepdims=True)
        probs = (expo / denom).astype(HALF_TYPE)
        lse_parts.append(peak + jnp.log(denom))
        head_out = jnp.dot(probs, value_cols, preferred_element_type=FULL_TYPE).astype(HALF_TYPE)
        mixed_parts.append(head_out.reshape(group_size, rows_here, HD).transpose(1, 0, 2))
    mixed = jnp.concatenate(mixed_parts, axis=1).reshape(rows_here, local_q * HD)
    attn_part = jnp.einsum("tc,dc->td", mixed, full_o, preferred_element_type=FULL_TYPE)
    attended = lax.psum(attn_part.astype(jnp.bfloat16), "tensor").astype(jnp.float32)
    resid = rows + attended
    scale_two = rms_scale(resid)
    unit_two = resid * scale_two
    second = (unit_two * gain_two).astype(HALF_TYPE)
    gate_up = jnp.dot(second, full_gu, preferred_element_type=FULL_TYPE)
    gate = gate_up[:, :width_f]
    up_proj = gate_up[:, width_f:]
    sigmoid_gate = jax.nn.sigmoid(gate)
    swish = gate * sigmoid_gate
    hidden = (swish * up_proj).astype(HALF_TYPE)
    ffn_part = jnp.einsum("tf,df->td", hidden, full_d, preferred_element_type=FULL_TYPE)
    d_hidden = jnp.dot(cotangent, full_d, preferred_element_type=FULL_TYPE)
    grad_down = jnp.einsum("td,tf->df", cotangent, hidden, preferred_element_type=FULL_TYPE)
    d_gate = (d_hidden * up_proj * sigmoid_gate * (1.0 + gate * (1.0 - sigmoid_gate))).astype(
        HALF_TYPE
    )
    d_up = (d_hidden * swish).astype(HALF_TYPE)
    d_gate_up = jnp.concatenate([d_gate, d_up], axis=1)
    grad_gate_up = jnp.einsum("td,tf->df", second, d_gate_up, preferred_element_type=FULL_TYPE)
    wide_grad = lax.psum_scatter(
        jnp.concatenate(
            [grad_gate_up.astype(jnp.bfloat16), grad_down.astype(jnp.bfloat16)], axis=1
        ),
        plane,
        scatter_dimension=0,
        tiled=True,
    ).astype(jnp.float32)
    d_second_part = jnp.einsum(
        "tf,df->td", d_gate_up, full_gu, preferred_element_type=FULL_TYPE
    )
    d_second = lax.psum(d_second_part.astype(jnp.bfloat16), "tensor").astype(jnp.float32)
    ffn_half, d_second = lax.optimization_barrier((ffn_part.astype(jnp.bfloat16), d_second))
    ffn_out = lax.psum(ffn_half, "tensor").astype(jnp.float32)
    block_out = (resid + ffn_out).astype(HALF_TYPE)
    d_resid = cotangent.astype(FULL_TYPE) + norm_back(d_second, unit_two, scale_two, gain_two)
    grad_gain_two = jnp.sum(d_second * unit_two, axis=0)
    d_attn = d_resid.astype(HALF_TYPE)
    grad_out = jnp.einsum("td,tc->dc", d_attn, mixed, preferred_element_type=FULL_TYPE)
    d_mixed = (
        jnp.dot(d_attn, full_o, preferred_element_type=FULL_TYPE)
        .astype(HALF_TYPE)
        .reshape(rows_here, local_q, HD)
    )
    d_query_parts = []
    d_key_parts = []
    d_value_parts = []
    for head_index in range(local_kv):
        query_rows = head_rows(query_half, head_index, group_size)
        grad_rows = head_rows(d_mixed, head_index, group_size)
        key_cols = key_all[:, head_index * HD : (head_index + 1) * HD]
        value_cols = value_all[:, head_index * HD : (head_index + 1) * HD]
        scores = head_scores(query_rows, key_cols)
        probs_full = jnp.exp(scores - lse_parts[head_index])
        probs_half = probs_full.astype(HALF_TYPE)
        d_probs = jnp.einsum("qd,kd->qk", grad_rows, value_cols, preferred_element_type=FULL_TYPE)
        delta = jnp.sum(probs_full * d_probs, axis=-1, keepdims=True)
        d_scores = (probs_full * (d_probs - delta)).astype(HALF_TYPE)
        d_query_rows = jnp.dot(d_scores, key_cols, preferred_element_type=FULL_TYPE) * scale
        d_query_parts.append(d_query_rows.reshape(group_size, rows_here, HD).transpose(1, 0, 2))
        d_key_parts.append(
            jnp.einsum("qk,qd->kd", d_scores, query_rows, preferred_element_type=FULL_TYPE) * scale
        )
        d_value_parts.append(
            jnp.einsum("qk,qd->kd", probs_half, grad_rows, preferred_element_type=FULL_TYPE)
        )
    d_key_all = jnp.concatenate(d_key_parts, axis=1)
    d_value_all = jnp.concatenate(d_value_parts, axis=1)
    key_value_grad = lax.psum_scatter(
        jnp.concatenate([d_key_all, d_value_all], axis=1).astype(jnp.bfloat16),
        "context",
        scatter_dimension=0,
        tiled=True,
    ).astype(jnp.float32)
    key_grad = key_value_grad[:, :width_k]
    value_grad = key_value_grad[:, width_k:]
    d_value_raw = value_grad.astype(HALF_TYPE)
    d_key_normed = rotate_back(key_grad.reshape(rows_here, local_kv, HD), cosines, sines_table)
    grad_gain_key = jnp.sum(d_key_normed * unit_k, axis=(0, 1))
    d_key_raw = (
        norm_back(d_key_normed, unit_k, scale_k, gain_key)
        .astype(HALF_TYPE)
        .reshape(rows_here, local_kv * HD)
    )
    d_query_normed = rotate_back(jnp.concatenate(d_query_parts, axis=1), cosines, sines_table)
    grad_gain_query = jnp.sum(d_query_normed * unit_q, axis=(0, 1))
    d_query_raw = (
        norm_back(d_query_normed, unit_q, scale_q, gain_query)
        .astype(HALF_TYPE)
        .reshape(rows_here, local_q * HD)
    )
    d_qkv = jnp.concatenate([d_query_raw, d_key_raw, d_value_raw], axis=1)
    grad_qkv = jnp.einsum("td,tc->dc", normed, d_qkv, preferred_element_type=FULL_TYPE)
    narrow_grad = lax.psum_scatter(
        jnp.concatenate([grad_qkv.astype(jnp.bfloat16), grad_out.astype(jnp.bfloat16)], axis=1),
        plane,
        scatter_dimension=0,
        tiled=True,
    ).astype(jnp.float32)
    d_normed_part = jnp.einsum("tc,dc->td", d_qkv, full_qkv, preferred_element_type=FULL_TYPE)
    d_normed_half, block_out = lax.optimization_barrier(
        (d_normed_part.astype(jnp.bfloat16), block_out)
    )
    d_normed = lax.psum(d_normed_half, "tensor").astype(jnp.float32)
    input_grad = d_resid + norm_back(d_normed, unit_one, scale_one, gain_one)
    grad_gain_one = jnp.sum(d_normed * unit_one, axis=0)
    first_tensor = (lax.axis_index("tensor") == 0).astype(FULL_TYPE)
    gain_local = jnp.concatenate(
        [grad_gain_one * first_tensor, grad_gain_two * first_tensor, grad_gain_query, grad_gain_key]
    )
    gain_total = lax.psum(gain_local, ("fsdp", "context", "tensor"))
    reduced = (
        narrow_grad[:, :width_q],
        narrow_grad[:, width_q : width_q + width_k],
        narrow_grad[:, width_q + width_k : width_q + 2 * width_k],
        narrow_grad[:, width_q + 2 * width_k :],
        wide_grad[:, :width_f],
        wide_grad[:, width_f : 2 * width_f],
        wide_grad[:, 2 * width_f :],
    )
    new_moments = tuple(
        (MU * moment_old + gradient for moment_old, gradient in zip(moments, reduced))
    )
    row_block = w_gate.shape[0]
    plane_size = lax.axis_size("fsdp") * context_size
    plane_index = lax.axis_index("fsdp") * context_size + lax.axis_index("context")
    wide_all = lax.all_gather(
        jnp.concatenate([moment.astype(HALF_TYPE) for moment in new_moments[4:]], axis=1),
        plane,
        axis=0,
        tiled=True,
    )
    wide_rows = lax.dynamic_slice_in_dim(wide_all, plane_index * row_block, row_block)
    wide = [wide_all[:, index * width_f : (index + 1) * width_f] for index in range(3)]
    gram_rows = jnp.stack(
        [
            lax.dot_general(
                wide_rows[:, index * width_f : (index + 1) * width_f],
                wide[index],
                (((1,), (1,)), ((), ())),
                preferred_element_type=FULL_TYPE,
            )
            for index in range(3)
        ]
    )
    gram_rows = lax.psum(gram_rows, "tensor").astype(HALF_TYPE)
    gram = lax.all_to_all(
        jnp.concatenate(
            [gram_rows, jnp.zeros((plane_size - 3, row_block, D), HALF_TYPE)], axis=0
        ),
        plane,
        split_axis=0,
        concat_axis=0,
        tiled=True,
    ).reshape(D, D)
    narrow = jnp.stack(
        [
            jnp.pad(moment.astype(HALF_TYPE), ((0, 0), (0, width_q - moment.shape[1])))
            for moment in new_moments[:4]
        ]
    )
    narrow_rows = (
        lax.all_to_all(narrow, "tensor", split_axis=0, concat_axis=0, tiled=True)
        .transpose(1, 0, 2)
        .reshape(row_block, tensor_size * width_q)
    )
    narrow_all = lax.all_gather(narrow_rows, plane, axis=0, tiled=True)
    ready = lax.cond(
        plane_index < 3,
        lambda gram_arg, narrow_arg: gram_newton_schulz(gram_arg),
        lambda gram_arg, narrow_arg: newton_schulz(narrow_arg),
        gram,
        narrow_all,
    )
    back_rows = lax.all_to_all(
        ready.reshape(plane_size, row_block, D), plane, split_axis=0, concat_axis=0, tiled=True
    )
    narrow_back = lax.all_to_all(
        back_rows[3].reshape(row_block, tensor_size, width_q).transpose(1, 0, 2),
        "tensor",
        split_axis=0,
        concat_axis=0,
        tiled=True,
    )
    ortho = [narrow_back[index, :, : masters[index].shape[1]] for index in range(4)] + [
        jnp.dot(back_rows[index], wide[index], preferred_element_type=FULL_TYPE).astype(HALF_TYPE)
        for index in range(3)
    ]
    new_weights = []
    for index in range(len(RATES)):
        columns = masters[index].shape[1]
        rate = RATES[index] * 0.2 * math.sqrt(max(D, columns * tensor_size))
        new_weights.append(masters[index] - rate * ortho[index].astype(FULL_TYPE))
    gain_mom = MU_G * gain_moment + gain_total
    new_gains = gains - LR_G * gain_mom
    return (
        block_out,
        input_grad,
        new_moments[0],
        new_moments[1],
        new_moments[2],
        new_moments[3],
        new_moments[4],
        new_moments[5],
        new_moments[6],
        new_weights[0],
        new_weights[1],
        new_weights[2],
        new_weights[3],
        new_weights[4],
        new_weights[5],
        new_weights[6],
        gain_mom,
        new_gains,
    )


def solution(mesh):
    in_specs = (
        P(("fsdp", "context"), None),
        P(("fsdp", "context"), None),
        P("fsdp", None),
        P(("fsdp", "context"), "tensor"),
        P(("fsdp", "context"), "tensor"),
        P(("fsdp", "context"), "tensor"),
        P(("fsdp", "context"), "tensor"),
        P(("fsdp", "context"), "tensor"),
        P(("fsdp", "context"), "tensor"),
        P(("fsdp", "context"), "tensor"),
        P(("fsdp", "context"), "tensor"),
        P(("fsdp", "context"), "tensor"),
        P(("fsdp", "context"), "tensor"),
        P(("fsdp", "context"), "tensor"),
        P(("fsdp", "context"), "tensor"),
        P(("fsdp", "context"), "tensor"),
        P(("fsdp", "context"), "tensor"),
        P(),
        P(),
    )
    out_specs = (
        P(("fsdp", "context"), None),
        P(("fsdp", "context"), None),
        P(("fsdp", "context"), "tensor"),
        P(("fsdp", "context"), "tensor"),
        P(("fsdp", "context"), "tensor"),
        P(("fsdp", "context"), "tensor"),
        P(("fsdp", "context"), "tensor"),
        P(("fsdp", "context"), "tensor"),
        P(("fsdp", "context"), "tensor"),
        P(("fsdp", "context"), "tensor"),
        P(("fsdp", "context"), "tensor"),
        P(("fsdp", "context"), "tensor"),
        P(("fsdp", "context"), "tensor"),
        P(("fsdp", "context"), "tensor"),
        P(("fsdp", "context"), "tensor"),
        P(("fsdp", "context"), "tensor"),
        P(),
        P(),
    )
    return jax.shard_map(body, mesh=mesh, in_specs=in_specs, out_specs=out_specs, check_vma=False)
```

```python
import math

import jax
import jax.numpy as jnp
from jax import lax
from jax.sharding import PartitionSpec as P

D = 1024
HEADS = 16
KV_HEADS = 8
HD = 64
NS_STEPS = 5


EPS = 1e-06
THETA = 1000000.0
MU = 0.95
MU_G = 0.9
LR_G = 0.001
NS_A = 3.4445
NS_B = -4.775
NS_C = 2.0315
RATES = (0.1, 0.1, 0.1, 0.8, 0.1, 0.1, 0.1)
FULL_TYPE = jnp.float32
HALF_TYPE = jnp.bfloat16


def rms_scale(values):
    return lax.rsqrt(jnp.mean(values * values, axis=-1, keepdims=True) + EPS)


def rotate(values, cosines, sines_table):
    half_dim = values.shape[-1] // 2
    front_half = values[..., :half_dim]
    back_half = values[..., half_dim:]
    cos_rows = cosines[:, None, :]
    sin_rows = sines_table[:, None, :]
    return jnp.concatenate(
        [
            front_half * cos_rows - back_half * sin_rows,
            back_half * cos_rows + front_half * sin_rows,
        ],
        axis=-1,
    )


def rotate_back(values, cosines, sines_table):
    half_dim = values.shape[-1] // 2
    front_half = values[..., :half_dim]
    back_half = values[..., half_dim:]
    cos_rows = cosines[:, None, :]
    sin_rows = sines_table[:, None, :]
    return jnp.concatenate(
        [
            front_half * cos_rows + back_half * sin_rows,
            back_half * cos_rows - front_half * sin_rows,
        ],
        axis=-1,
    )


def norm_back(upstream, unit_rows, scale_rows, gain_row):
    scaled = upstream * gain_row
    return scale_rows * (scaled - unit_rows * jnp.mean(scaled * unit_rows, axis=-1, keepdims=True))


def stream_layout(row_lengths, points):
    ends = jnp.cumsum(row_lengths)
    after = (points[:, None] >= ends[None, :]).astype(jnp.int32)
    segment = jnp.sum(after, axis=1)
    place = points - jnp.sum(after * row_lengths[None, :], axis=1)
    return (segment, place)


def rope_tables(place):
    freq = THETA ** (-(2.0 * jnp.arange(HD // 2, dtype=FULL_TYPE)) / HD)
    angles = place.astype(FULL_TYPE)[:, None] * freq[None, :]
    return (jnp.cos(angles), jnp.sin(angles))


def newton_schulz(matrix):
    wide = matrix.astype(FULL_TYPE)
    frob_norm = jnp.sqrt(jnp.sum(wide * wide))
    current = (wide / (frob_norm + 1e-07)).astype(HALF_TYPE)
    for repeat in range(NS_STEPS):
        square = lax.dot_general(
            current, current, (((1,), (1,)), ((), ())), preferred_element_type=FULL_TYPE
        ).astype(HALF_TYPE)
        quartic = jnp.dot(square, square, preferred_element_type=FULL_TYPE)
        mixer = (NS_B * square.astype(FULL_TYPE) + NS_C * quartic).astype(HALF_TYPE)
        current = (
            NS_A * current.astype(FULL_TYPE)
            + jnp.dot(mixer, current, preferred_element_type=FULL_TYPE)
        ).astype(HALF_TYPE)
    return current


def gram_newton_schulz(gram_half):
    gram = gram_half.astype(FULL_TYPE)
    size = gram.shape[0]
    diagonal = jnp.arange(size)[:, None] == jnp.arange(size)[None, :]
    norm = jnp.sqrt(jnp.sum(jnp.where(diagonal, gram, 0.0))) + 1e-07
    inverse = 1.0 / norm
    gram = gram * inverse * inverse
    total = None
    for repeat in range(NS_STEPS):
        half = gram.astype(HALF_TYPE)
        mixer_full = NS_B * gram + NS_C * jnp.dot(half, half, preferred_element_type=FULL_TYPE)
        mixer = mixer_full.astype(HALF_TYPE)
        if total is None:
            total = jnp.where(diagonal, NS_A, 0.0) + mixer_full
        else:
            total = NS_A * total + jnp.dot(
                mixer, total.astype(HALF_TYPE), preferred_element_type=FULL_TYPE
            )
        if repeat < NS_STEPS - 1:
            once = NS_A * gram + jnp.dot(mixer, half, preferred_element_type=FULL_TYPE)
            gram = NS_A * once + jnp.dot(
                once.astype(HALF_TYPE), mixer, preferred_element_type=FULL_TYPE
            )
    return (total * inverse).astype(HALF_TYPE)


def swap(values, axis, bit):
    return lax.ppermute(values, axis, [(i, i ^ bit) for i in range(lax.axis_size(axis))])


def bits_of(axis):
    size = lax.axis_size(axis)
    return [(axis, 1 << power) for power in reversed(range(size.bit_length() - 1))]


def plane_gather(shard):
    along = bits_of("context")
    context_size = lax.axis_size("context")
    block = shard[None]
    offsets = [0]
    for axis, bit in along[:-1] + bits_of("fsdp") + along[-1:]:
        other = swap(block, axis, bit)
        weight = context_size * bit if axis == "fsdp" else bit
        block = jnp.concatenate([block, other], axis=0)
        offsets = offsets + [offset ^ weight for offset in offsets]
    here = lax.axis_index("fsdp") * context_size + lax.axis_index("context")
    rows = shard.shape[0]
    whole = jnp.zeros((rows * len(offsets), shard.shape[1]), shard.dtype)
    for position, offset in enumerate(offsets):
        start = lax.bitwise_xor(here, offset) * rows
        whole = lax.dynamic_update_slice_in_dim(whole, block[position], start, axis=0)
    return whole


def swapped_sum(values):
    for axis in ("context", "fsdp", "tensor"):
        for name, bit in bits_of(axis):
            values = values + swap(values, name, bit)
    return values


def scatter_sum(values, axes, pieces):
    parts = values.reshape(pieces, values.shape[0] // pieces, values.shape[1])
    arrived = lax.all_to_all(parts, axes, split_axis=0, concat_axis=0, tiled=True)
    return jnp.sum(arrived.astype(FULL_TYPE), axis=0)


def head_rows(values, head_index, group_size):
    picked = values[:, head_index * group_size : (head_index + 1) * group_size, :]
    return picked.transpose(1, 0, 2).reshape(group_size * values.shape[0], values.shape[2])


def body(
    inputs,
    cotangent,
    lengths,
    w_query,
    w_key,
    w_value,
    w_out,
    w_gate,
    w_up,
    w_down,
    m_query,
    m_key,
    m_value,
    m_out,
    m_gate,
    m_up,
    m_down,
    gains,
    gain_moment,
):
    masters = (w_query, w_key, w_value, w_out, w_gate, w_up, w_down)
    moments = (m_query, m_key, m_value, m_out, m_gate, m_up, m_down)
    rows_here = inputs.shape[0]
    context_size = lax.axis_size("context")
    tensor_size = lax.axis_size("tensor")
    span = context_size * rows_here
    offset = lax.axis_index("context") * rows_here
    local_q = w_query.shape[1] // HD
    local_kv = w_key.shape[1] // HD
    group_size = HEADS // KV_HEADS
    scale = HD ** (-0.5)
    gain_one = gains[:D]
    gain_two = gains[D : 2 * D]
    gain_query = gains[2 * D : 2 * D + HD]
    gain_key = gains[2 * D + HD :]
    points = jnp.arange(span, dtype=jnp.int32)
    segment, place = stream_layout(lengths[0], points)
    query_points = offset + jnp.arange(rows_here, dtype=jnp.int32)
    query_segment = lax.dynamic_slice_in_dim(segment, offset, rows_here)
    query_place = lax.dynamic_slice_in_dim(place, offset, rows_here)
    allowed = (query_segment[:, None] == segment[None, :]) & (
        points[None, :] <= query_points[:, None]
    )
    allowed_rows = jnp.concatenate([allowed] * group_size, axis=0)
    cosines, sines_table = rope_tables(query_place)
    half_q = w_query.astype(HALF_TYPE)
    half_k = w_key.astype(HALF_TYPE)
    half_v = w_value.astype(HALF_TYPE)
    half_o = w_out.astype(HALF_TYPE)
    half_g = w_gate.astype(HALF_TYPE)
    half_u = w_up.astype(HALF_TYPE)
    half_d = w_down.astype(HALF_TYPE)
    plane = ("fsdp", "context")
    width_q, width_k, width_f = w_query.shape[1], w_key.shape[1], w_gate.shape[1]
    full_qkvo = lax.all_gather(
        jnp.concatenate([half_q, half_k, half_v, half_o], axis=1), plane, axis=0, tiled=True
    )
    full_qkv = full_qkvo[:, : width_q + 2 * width_k]
    full_o = full_qkvo[:, width_q + 2 * width_k :]
    wide_half, full_qkv = lax.optimization_barrier(
        (jnp.concatenate([half_g, half_u, half_d], axis=1), full_qkv)
    )
    full_gud = plane_gather(wide_half)
    full_gu = full_gud[:, : 2 * width_f]
    full_d = full_gud[:, 2 * width_f :]
    rows = inputs.astype(FULL_TYPE)
    scale_one = rms_scale(rows)
    unit_one = rows * scale_one
    normed = (unit_one * gain_one).astype(HALF_TYPE)
    qkv_raw = jnp.dot(normed, full_qkv, preferred_element_type=FULL_TYPE)
    query_raw = qkv_raw[:, :width_q].reshape(rows_here, local_q, HD)
    key_raw = qkv_raw[:, width_q : width_q + width_k].reshape(rows_here, local_kv, HD)
    value_half = qkv_raw[:, width_q + width_k :].astype(HALF_TYPE)
    scale_q = rms_scale(query_raw)
    unit_q = query_raw * scale_q
    query_half = rotate(unit_q * gain_query, cosines, sines_table).astype(HALF_TYPE)
    scale_k = rms_scale(key_raw)
    unit_k = key_raw * scale_k
    key_half = rotate(unit_k * gain_key, cosines, sines_table).astype(HALF_TYPE)
    key_value = lax.all_gather(
        jnp.concatenate([key_half.reshape(rows_here, local_kv * HD), value_half], axis=1),
        "context",
        axis=0,
        tiled=True,
    )
    key_all = key_value[:, :width_k]
    value_all = key_value[:, width_k:]

    def head_scores(query_rows, key_cols):
        scores = (
            jnp.einsum("qd,kd->qk", query_rows, key_cols, preferred_element_type=FULL_TYPE) * scale
        )
        return jnp.where(allowed_rows, scores, -1e30)

    mixed_parts = []
    lse_parts = []
    for head_index in range(local_kv):
        query_rows = head_rows(query_half, head_index, group_size)
        key_cols = key_all[:, head_index * HD : (head_index + 1) * HD]
        value_cols = value_all[:, head_index * HD : (head_index + 1) * HD]
        scores = head_scores(query_rows, key_cols)
        peak = jnp.max(scores, axis=-1, keepdims=True)
        expo = jnp.exp(scores - peak)
        denom = jnp.sum(expo, axis=-1, keepdims=True)
        probs = (expo / denom).astype(HALF_TYPE)
        lse_parts.append(peak + jnp.log(denom))
        head_out = jnp.dot(probs, value_cols, preferred_element_type=FULL_TYPE).astype(HALF_TYPE)
        mixed_parts.append(head_out.reshape(group_size, rows_here, HD).transpose(1, 0, 2))
    mixed = jnp.concatenate(mixed_parts, axis=1).reshape(rows_here, local_q * HD)
    attn_part = jnp.einsum("tc,dc->td", mixed, full_o, preferred_element_type=FULL_TYPE)
    attended = lax.psum(attn_part.astype(jnp.bfloat16), "tensor").astype(jnp.float32)
    resid = rows + attended
    scale_two = rms_scale(resid)
    unit_two = resid * scale_two
    second = (unit_two * gain_two).astype(HALF_TYPE)
    gate_up = jnp.dot(second, full_gu, preferred_element_type=FULL_TYPE)
    gate = gate_up[:, :width_f]
    up_proj = gate_up[:, width_f:]
    sigmoid_gate = jax.nn.sigmoid(gate)
    swish = gate * sigmoid_gate
    hidden = (swish * up_proj).astype(HALF_TYPE)
    ffn_part = jnp.einsum("tf,df->td", hidden, full_d, preferred_element_type=FULL_TYPE)
    d_hidden = jnp.dot(cotangent, full_d, preferred_element_type=FULL_TYPE)
    grad_down = jnp.einsum("td,tf->df", cotangent, hidden, preferred_element_type=FULL_TYPE)
    d_gate = (d_hidden * up_proj * sigmoid_gate * (1.0 + gate * (1.0 - sigmoid_gate))).astype(
        HALF_TYPE
    )
    d_up = (d_hidden * swish).astype(HALF_TYPE)
    d_gate_up = jnp.concatenate([d_gate, d_up], axis=1)
    grad_gate_up = jnp.einsum("td,tf->df", second, d_gate_up, preferred_element_type=FULL_TYPE)
    wide_part = jnp.concatenate(
        [grad_gate_up.astype(jnp.bfloat16), grad_down.astype(jnp.bfloat16)], axis=1
    )
    d_second_part = jnp.einsum(
        "tf,df->td", d_gate_up, full_gu, preferred_element_type=FULL_TYPE
    )
    d_second = lax.psum(d_second_part.astype(jnp.bfloat16), "tensor").astype(jnp.float32)
    wide_part, d_second = lax.optimization_barrier((wide_part, d_second))
    wide_grad = lax.psum_scatter(
        wide_part, plane, scatter_dimension=0, tiled=True
    ).astype(jnp.float32)
    d_resid = cotangent.astype(FULL_TYPE) + norm_back(d_second, unit_two, scale_two, gain_two)
    grad_gain_two = jnp.sum(d_second * unit_two, axis=0)
    d_attn = d_resid.astype(HALF_TYPE)
    grad_out = jnp.einsum("td,tc->dc", d_attn, mixed, preferred_element_type=FULL_TYPE)
    d_mixed = (
        jnp.dot(d_attn, full_o, preferred_element_type=FULL_TYPE)
        .astype(HALF_TYPE)
        .reshape(rows_here, local_q, HD)
    )
    d_query_parts = []
    d_key_parts = []
    d_value_parts = []
    for head_index in range(local_kv):
        query_rows = head_rows(query_half, head_index, group_size)
        grad_rows = head_rows(d_mixed, head_index, group_size)
        key_cols = key_all[:, head_index * HD : (head_index + 1) * HD]
        value_cols = value_all[:, head_index * HD : (head_index + 1) * HD]
        scores = head_scores(query_rows, key_cols)
        probs_full = jnp.exp(scores - lse_parts[head_index])
        probs_half = probs_full.astype(HALF_TYPE)
        d_probs = jnp.einsum("qd,kd->qk", grad_rows, value_cols, preferred_element_type=FULL_TYPE)
        delta = jnp.sum(probs_full * d_probs, axis=-1, keepdims=True)
        d_scores = (probs_full * (d_probs - delta)).astype(HALF_TYPE)
        d_query_rows = jnp.dot(d_scores, key_cols, preferred_element_type=FULL_TYPE) * scale
        d_query_parts.append(d_query_rows.reshape(group_size, rows_here, HD).transpose(1, 0, 2))
        d_key_parts.append(
            jnp.einsum("qk,qd->kd", d_scores, query_rows, preferred_element_type=FULL_TYPE) * scale
        )
        d_value_parts.append(
            jnp.einsum("qk,qd->kd", probs_half, grad_rows, preferred_element_type=FULL_TYPE)
        )
    d_key_all = jnp.concatenate(d_key_parts, axis=1)
    d_value_all = jnp.concatenate(d_value_parts, axis=1)
    key_value_grad = scatter_sum(
        jnp.concatenate([d_key_all, d_value_all], axis=1).astype(jnp.bfloat16),
        "context",
        context_size,
    )
    key_grad = key_value_grad[:, :width_k]
    value_grad = key_value_grad[:, width_k:]
    d_value_raw = value_grad.astype(HALF_TYPE)
    d_key_normed = rotate_back(key_grad.reshape(rows_here, local_kv, HD), cosines, sines_table)
    grad_gain_key = jnp.sum(d_key_normed * unit_k, axis=(0, 1))
    d_key_raw = (
        norm_back(d_key_normed, unit_k, scale_k, gain_key)
        .astype(HALF_TYPE)
        .reshape(rows_here, local_kv * HD)
    )
    d_query_normed = rotate_back(jnp.concatenate(d_query_parts, axis=1), cosines, sines_table)
    grad_gain_query = jnp.sum(d_query_normed * unit_q, axis=(0, 1))
    d_query_raw = (
        norm_back(d_query_normed, unit_q, scale_q, gain_query)
        .astype(HALF_TYPE)
        .reshape(rows_here, local_q * HD)
    )
    d_qkv = jnp.concatenate([d_query_raw, d_key_raw, d_value_raw], axis=1)
    grad_qkv = jnp.einsum("td,tc->dc", normed, d_qkv, preferred_element_type=FULL_TYPE)
    plane_size = lax.axis_size("fsdp") * context_size
    narrow_grad = scatter_sum(
        jnp.concatenate([grad_qkv.astype(jnp.bfloat16), grad_out.astype(jnp.bfloat16)], axis=1),
        plane,
        plane_size,
    )
    d_normed_part = jnp.einsum("tc,dc->td", d_qkv, full_qkv, preferred_element_type=FULL_TYPE)
    d_normed = lax.psum(d_normed_part.astype(jnp.bfloat16), "tensor").astype(jnp.float32)
    ffn_half, d_normed = lax.optimization_barrier((ffn_part.astype(jnp.bfloat16), d_normed))
    ffn_out = lax.psum(ffn_half, "tensor").astype(jnp.float32)
    block_out = (resid + ffn_out).astype(HALF_TYPE)
    input_grad = d_resid + norm_back(d_normed, unit_one, scale_one, gain_one)
    grad_gain_one = jnp.sum(d_normed * unit_one, axis=0)
    first_tensor = (lax.axis_index("tensor") == 0).astype(FULL_TYPE)
    gain_local = jnp.concatenate(
        [grad_gain_one * first_tensor, grad_gain_two * first_tensor, grad_gain_query, grad_gain_key]
    )
    gain_total = swapped_sum(gain_local)
    reduced = (
        narrow_grad[:, :width_q],
        narrow_grad[:, width_q : width_q + width_k],
        narrow_grad[:, width_q + width_k : width_q + 2 * width_k],
        narrow_grad[:, width_q + 2 * width_k :],
        wide_grad[:, :width_f],
        wide_grad[:, width_f : 2 * width_f],
        wide_grad[:, 2 * width_f :],
    )
    new_moments = tuple(
        (MU * moment_old + gradient for moment_old, gradient in zip(moments, reduced))
    )
    row_block = w_gate.shape[0]
    plane_index = lax.axis_index("fsdp") * context_size + lax.axis_index("context")
    wide_all = lax.all_gather(
        jnp.concatenate([moment.astype(HALF_TYPE) for moment in new_moments[4:]], axis=1),
        plane,
        axis=0,
        tiled=True,
    )
    wide_rows = lax.dynamic_slice_in_dim(wide_all, plane_index * row_block, row_block)
    wide = [wide_all[:, index * width_f : (index + 1) * width_f] for index in range(3)]
    gram_rows = jnp.stack(
        [
            lax.dot_general(
                wide_rows[:, index * width_f : (index + 1) * width_f],
                wide[index],
                (((1,), (1,)), ((), ())),
                preferred_element_type=FULL_TYPE,
            )
            for index in range(3)
        ]
    )
    gram_piece = scatter_sum(
        gram_rows.reshape(3 * row_block, D).astype(HALF_TYPE), "tensor", tensor_size
    ).astype(HALF_TYPE)
    gram_rows = lax.all_to_all(
        jnp.broadcast_to(gram_piece[None], (tensor_size,) + gram_piece.shape),
        "tensor",
        split_axis=0,
        concat_axis=0,
        tiled=True,
    ).reshape(3, row_block, D)
    gram = lax.all_to_all(
        jnp.concatenate(
            [gram_rows, jnp.zeros((plane_size - 3, row_block, D), HALF_TYPE)], axis=0
        ),
        plane,
        split_axis=0,
        concat_axis=0,
        tiled=True,
    ).reshape(D, D)
    narrow = jnp.stack(
        [
            jnp.pad(moment.astype(HALF_TYPE), ((0, 0), (0, width_q - moment.shape[1])))
            for moment in new_moments[:4]
        ]
    )
    narrow_rows = (
        lax.all_to_all(narrow, "tensor", split_axis=0, concat_axis=0, tiled=True)
        .transpose(1, 0, 2)
        .reshape(row_block, tensor_size * width_q)
    )
    narrow_all = plane_gather(narrow_rows)
    ready = lax.cond(
        plane_index < 3,
        lambda gram_arg, narrow_arg: gram_newton_schulz(gram_arg),
        lambda gram_arg, narrow_arg: newton_schulz(narrow_arg),
        gram,
        narrow_all,
    )
    back_rows = lax.all_to_all(
        ready.reshape(plane_size, row_block, D), plane, split_axis=0, concat_axis=0, tiled=True
    )
    narrow_back = lax.all_to_all(
        back_rows[3].reshape(row_block, tensor_size, width_q).transpose(1, 0, 2),
        "tensor",
        split_axis=0,
        concat_axis=0,
        tiled=True,
    )
    ortho = [narrow_back[index, :, : masters[index].shape[1]] for index in range(4)] + [
        jnp.dot(back_rows[index], wide[index], preferred_element_type=FULL_TYPE).astype(HALF_TYPE)
        for index in range(3)
    ]
    new_weights = []
    for index in range(len(RATES)):
        columns = masters[index].shape[1]
        rate = RATES[index] * 0.2 * math.sqrt(max(D, columns * tensor_size))
        new_weights.append(masters[index] - rate * ortho[index].astype(FULL_TYPE))
    gain_mom = MU_G * gain_moment + gain_total
    new_gains = gains - LR_G * gain_mom
    return (
        block_out,
        input_grad,
        new_moments[0],
        new_moments[1],
        new_moments[2],
        new_moments[3],
        new_moments[4],
        new_moments[5],
        new_moments[6],
        new_weights[0],
        new_weights[1],
        new_weights[2],
        new_weights[3],
        new_weights[4],
        new_weights[5],
        new_weights[6],
        gain_mom,
        new_gains,
    )


def solution(mesh):
    in_specs = (
        P(("fsdp", "context"), None),
        P(("fsdp", "context"), None),
        P("fsdp", None),
        P(("fsdp", "context"), "tensor"),
        P(("fsdp", "context"), "tensor"),
        P(("fsdp", "context"), "tensor"),
        P(("fsdp", "context"), "tensor"),
        P(("fsdp", "context"), "tensor"),
        P(("fsdp", "context"), "tensor"),
        P(("fsdp", "context"), "tensor"),
        P(("fsdp", "context"), "tensor"),
        P(("fsdp", "context"), "tensor"),
        P(("fsdp", "context"), "tensor"),
        P(("fsdp", "context"), "tensor"),
        P(("fsdp", "context"), "tensor"),
        P(("fsdp", "context"), "tensor"),
        P(("fsdp", "context"), "tensor"),
        P(),
        P(),
    )
    out_specs = (
        P(("fsdp", "context"), None),
        P(("fsdp", "context"), None),
        P(("fsdp", "context"), "tensor"),
        P(("fsdp", "context"), "tensor"),
        P(("fsdp", "context"), "tensor"),
        P(("fsdp", "context"), "tensor"),
        P(("fsdp", "context"), "tensor"),
        P(("fsdp", "context"), "tensor"),
        P(("fsdp", "context"), "tensor"),
        P(("fsdp", "context"), "tensor"),
        P(("fsdp", "context"), "tensor"),
        P(("fsdp", "context"), "tensor"),
        P(("fsdp", "context"), "tensor"),
        P(("fsdp", "context"), "tensor"),
        P(("fsdp", "context"), "tensor"),
        P(("fsdp", "context"), "tensor"),
        P(),
        P(),
    )
    return jax.shard_map(body, mesh=mesh, in_specs=in_specs, out_specs=out_specs, check_vma=False)
```
